128 devices in a mesh: sub: 16 (over x, y), code: 8 (over z, core).
Axes of the slice: x: 4, y: 4, z: 4, core: 2. Of those that a mesh axis runs over, the one named last changes fastest.
Arguments:
- inputs: bfloat16 [4096, 1024], P('sub'), may hold values from -6 to 6
- upstream: bfloat16 [4096, 1024], P('sub'), may hold values from -6 to 6
- codebook: bfloat16 [16, 64, 32768], P('sub', None, 'code'), may hold values from -8 to 8
Outputs:
- quantized: bfloat16 [4096, 1024], P('sub')
- grad_inputs: bfloat16 [4096, 1024], P('sub')
- grad_codebook: float32 [16, 64, 32768], P('sub', None, 'code')
The draws below stay inside these ranges and needn't reach their ends.
All inputs are finite; a program needn't handle non-finite values.
Results may differ from the reference program's by a relative error of at most 0.012.
Values may be sent and summed in bfloat16 or wider, within the bound.
No kernel may reach another device: no remote copies, remote signals or barrier semaphores. Data moves between devices by JAX's collectives and lax.ppermute only.
A program may use at most 256 MiB of HBM per device.

```python
import jax
import jax.numpy as jnp
from jax import lax

M = 16
DS = 64
K = 32768
D = 1024
ROWS = 4096
N_CODE = 8


def draw_inputs(key, part):
    key = jax.random.fold_in(key, 11)
    base = jax.random.truncated_normal(key, -5.0, 5.0, (ROWS, D), jnp.float32)
    return base.astype(jnp.bfloat16)


def draw_codebook(key, part):
    key = jax.random.fold_in(key, 23)
    base = 2.0 * jax.random.truncated_normal(key, -4.0, 4.0, (M, DS, K), jnp.float32)
    return base.astype(jnp.bfloat16)


def block_scale(rng, shape, shards, least, top_value):
    gain, own = 1.0, jax.random.fold_in(rng, 6)
    for axis_at, blocks in shards:
        steps = jnp.exp(jax.random.uniform(jax.random.fold_in(own, axis_at), (blocks,), jnp.float32, least / len(shards), top_value / len(shards)))
        gain = gain * jnp.repeat(steps, shape[axis_at] // blocks).reshape([-1 if axis == axis_at else 1 for axis in range(len(shape))])
    return gain


def scatter_about(rng, extent, scale, most, cuts=(), kind=jnp.bfloat16):
    result = scale * jax.random.normal(rng, extent, jnp.float32)
    if cuts:
        result = result * block_scale(rng, extent, cuts, -0.22, 0.18)
    return jnp.clip(result, -most, most).astype(kind)


def setup_inputs(seed: int = 0) -> dict:
    arg_keys = jax.random.split(jax.random.key(seed), 4)
    return {
        "inputs": draw_inputs(jax.random.fold_in(arg_keys[3], 71), 0),
        "upstream": scatter_about(arg_keys[1], (ROWS, D), 1.0, 6.0, ((0, 16),)),
        "codebook": draw_codebook(jax.random.fold_in(arg_keys[3], 71), 0),
    }


score_scale = 0.25


def one_subspace(inputs, upstream, codebook, index):
    rows = inputs.shape[0]
    blk = 512 if rows % 512 == 0 else rows
    start = (index * DS).astype(jnp.int32)
    x_sub = lax.dynamic_slice_in_dim(inputs, start, DS, 1)
    g_sub = lax.dynamic_slice_in_dim(upstream, start, DS, 1)
    book = lax.dynamic_index_in_dim(codebook, index, 0, keepdims=False)
    width = K // N_CODE
    book_blocks = book.reshape(DS, N_CODE, width).astype(jnp.float32)

    def step(acc, item):
        xb, gb = item
        scores = score_scale * jnp.dot(xb, book, preferred_element_type=jnp.float32)
        split = scores.reshape(blk, N_CODE, width)
        top_c = jnp.max(split, axis=2)
        expo = jnp.exp(split - top_c[:, :, None])
        total_c = jnp.sum(expo, axis=2)
        rounded = expo.astype(jnp.bfloat16).astype(jnp.float32)
        part_c = jnp.einsum("bnk,dnk->bnd", rounded, book_blocks)
        top = jnp.max(top_c, axis=1)
        factor = jnp.exp(top_c - top[:, None])
        total = jnp.sum(factor * total_c, axis=1)
        quant = jnp.sum(factor[:, :, None] * part_c, axis=1) / total[:, None]
        prob = jnp.exp(scores - top[:, None]) / total[:, None]
        dprob = jnp.dot(gb, book, preferred_element_type=jnp.float32)
        gq = jnp.sum(gb.astype(jnp.float32) * quant, axis=1)
        dscore = prob * (dprob - gq[:, None])
        dsb = dscore.astype(jnp.bfloat16)
        pb = prob.astype(jnp.bfloat16)
        dx = score_scale * jnp.dot(dsb, book.T, preferred_element_type=jnp.float32)
        dbook = score_scale * jnp.dot(xb.T, dsb, preferred_element_type=jnp.float32)
        dbook = dbook + jnp.dot(gb.T, pb, preferred_element_type=jnp.float32)
        return acc + dbook, (quant, dx)

    items = (x_sub.reshape(rows // blk, blk, DS), g_sub.reshape(rows // blk, blk, DS))
    dbook, (quant, dx) = lax.scan(step, jnp.zeros((DS, K), jnp.float32), items)
    return quant.reshape(rows, DS), dx.reshape(rows, DS), dbook


def reference(inputs, upstream, codebook):
    rows = inputs.shape[0]
    quant, dx, dbook = lax.map(lambda i: one_subspace(inputs, upstream, codebook, i), jnp.arange(M, dtype=jnp.int32))
    quantized = quant.transpose(1, 0, 2).reshape(rows, M * DS).astype(jnp.bfloat16)
    grad_inputs = dx.transpose(1, 0, 2).reshape(rows, M * DS).astype(jnp.bfloat16)
    return quantized, grad_inputs, dbook
```

```python
import functools

import jax
import jax.numpy as jnp
from jax import lax
from jax.experimental import pallas as pl
from jax.experimental.pallas import tpu as pltpu
from jax.sharding import PartitionSpec as P

BF16 = jnp.bfloat16
F32 = jnp.float32
DS = 64
LANES = 128
SCALE = 0.25
LOG2E = 1.4426950408889634
VMEM_LIMIT = 56 * 2**20


def scores_body(chunk, xa_ref, xb_ref, book_ref, bookt_ref, e_ref, part_ref, stat_ref, xgt_ref, s0, s1, m0, m1):
    t = pl.program_id(0)
    rows, codes = s0.shape

    def step(s_new, m_new, s_old, m_old):
        x = xa_ref[:, :DS]
        top = m_old[...]
        wide = jnp.concatenate([top] * (chunk // LANES), axis=1)
        most = None
        acc = jnp.zeros((rows, LANES), F32)
        for c in range(0, codes, chunk):
            s = jnp.dot(x, book_ref[:, c : c + chunk], preferred_element_type=F32)
            s_new[:, c : c + chunk] = s
            for k in range(0, chunk, LANES):
                piece = s[:, k : k + LANES]
                most = piece if most is None else jnp.maximum(most, piece)
            e = jnp.exp2(s_old[:, c : c + chunk] * (SCALE * LOG2E) - wide).astype(BF16)
            e_ref[:, c : c + chunk] = e
            acc = acc + jnp.dot(e, bookt_ref[c : c + chunk, :], preferred_element_type=F32)
        m_new[...] = jnp.broadcast_to(jnp.max(most, axis=1, keepdims=True) * (SCALE * LOG2E), (rows, LANES))
        part_ref[...] = acc
        lane = lax.broadcasted_iota(jnp.int32, (rows, LANES), 1)
        total = jnp.sum(jnp.where(lane == DS, acc, 0.0), axis=1, keepdims=True)
        g = xb_ref[:, DS:].astype(F32)
        h = jnp.sum(acc[:, :DS] * g, axis=1, keepdims=True)
        stat = jnp.where(lane == 0, top, jnp.where(lane == 1, total, h))
        stat_ref[...] = stat.T[:8]
        xgt_ref[...] = xb_ref[...].T

    @pl.when(t % 2 == 0)
    def _():
        step(s0, m0, s1, m1)

    @pl.when(t % 2 == 1)
    def _():
        step(s1, m1, s0, m0)


def scores(xg, book, bookt, tile=128, chunk=1024):
    rows, codes = xg.shape[0], book.shape[1]
    tiles = rows // tile
    now = lambda t: jnp.minimum(t, tiles - 1)
    old = lambda t: jnp.maximum(t - 1, 0)
    pairs = rows * codes
    return pl.pallas_call(
        functools.partial(scores_body, chunk),
        grid=(tiles + 1,),
        in_specs=[
            pl.BlockSpec((tile, LANES), lambda t: (now(t), 0)),
            pl.BlockSpec((tile, LANES), lambda t: (old(t), 0)),
            pl.BlockSpec((DS, codes), lambda t: (0, 0)),
            pl.BlockSpec((codes, LANES), lambda t: (0, 0)),
        ],
        out_specs=[
            pl.BlockSpec((tile, codes), lambda t: (old(t), 0)),
            pl.BlockSpec((tile, LANES), lambda t: (old(t), 0)),
            pl.BlockSpec((8, tile), lambda t: (0, old(t))),
            pl.BlockSpec((LANES, tile), lambda t: (0, old(t))),
        ],
        out_shape=[
            jax.ShapeDtypeStruct((rows, codes), BF16),
            jax.ShapeDtypeStruct((rows, LANES), F32),
            jax.ShapeDtypeStruct((8, rows), F32),
            jax.ShapeDtypeStruct((LANES, rows), BF16),
        ],
        scratch_shapes=[pltpu.VMEM((tile, codes), F32)] * 2 + [pltpu.VMEM((tile, LANES), F32)] * 2,
        compiler_params=pltpu.CompilerParams(vmem_limit_bytes=VMEM_LIMIT),
        cost_estimate=pl.CostEstimate(flops=pairs * 1024, bytes_accessed=pairs * 2, transcendentals=pairs),
        name="scores",
    )(xg, xg, book, bookt)


def slopes_body(chunk, xg_ref, book_ref, bookt_ref, e_ref, part_ref, own_ref, o1, o2, o3, ds_ref, out_ref, f_ref, d0, d1):
    rows, codes = e_ref.shape
    stats = [own_ref[...], o1[...], o2[...], o3[...]]
    top = functools.reduce(jnp.maximum, [s[0:1] for s in stats])
    rel = [jnp.exp2(s[0:1] - top) for s in stats]
    z = sum(r * s[1:2] for r, s in zip(rel, stats))
    gq_row = sum(r * s[2:3] for r, s in zip(rel, stats)) / z
    f_row = rel[0] / z
    f_ref[...] = jnp.broadcast_to(f_row, f_ref.shape)
    sub = lax.broadcasted_iota(jnp.int32, (LANES, rows), 0)
    turned = jnp.where(sub == 0, f_row, gq_row).T
    f = jnp.broadcast_to(turned[:, 0:1], (rows, LANES))
    gq = jnp.broadcast_to(turned[:, 1:2], (rows, LANES))
    wide = jnp.concatenate([gq] * (chunk // LANES), axis=1)

    g = xg_ref[:, DS:]
    acc = jnp.zeros((rows, LANES), F32)
    slots = [d0, d1]
    steps = codes // chunk
    for c in range(steps + 1):
        if c < steps:
            at = slice(c * chunk, (c + 1) * chunk)
            slots[c % 2][...] = jnp.dot(g, book_ref[:, at], preferred_element_type=F32) - wide
        if c > 0:
            at = slice((c - 1) * chunk, c * chunk)
            ds = (slots[(c - 1) % 2][...] * e_ref[:, at].astype(F32)).astype(BF16)
            ds_ref[:, at] = ds
            acc = acc + jnp.dot(ds, bookt_ref[at, :], preferred_element_type=F32)
    q = (part_ref[...] * f)[:, :DS]
    dx = (acc * (SCALE * f))[:, :DS]
    out_ref[...] = jnp.concatenate([q, dx], axis=1).astype(BF16)


def slopes(xg, book, bookt, e, part, stats, tile=256, chunk=1024):
    rows, codes = e.shape
    pairs = rows * codes
    by_row = lambda w: pl.BlockSpec((tile, w), lambda t: (t, 0))
    stat = pl.BlockSpec((8, tile), lambda t: (0, t))
    return pl.pallas_call(
        functools.partial(slopes_body, chunk),
        grid=(rows // tile,),
        in_specs=[
            by_row(LANES),
            pl.BlockSpec((DS, codes), lambda t: (0, 0)),
            pl.BlockSpec((codes, LANES), lambda t: (0, 0)),
            by_row(codes),
            by_row(LANES),
        ]
        + [stat] * 4,
        out_specs=[by_row(codes), by_row(LANES), stat],
        out_shape=[
            jax.ShapeDtypeStruct((rows, codes), BF16),
            jax.ShapeDtypeStruct((rows, LANES), BF16),
            jax.ShapeDtypeStruct((8, rows), F32),
        ],
        scratch_shapes=[pltpu.VMEM((tile, chunk), F32)] * 2,
        compiler_params=pltpu.CompilerParams(vmem_limit_bytes=VMEM_LIMIT),
        cost_estimate=pl.CostEstimate(flops=pairs * 1024, bytes_accessed=pairs * 4, transcendentals=0),
        name="slopes",
    )(xg, book, bookt, e, part, *stats)


def book_body(xgt_ref, f_ref, ds_ref, e_ref, out_ref, w_ref):
    @pl.when(pl.program_id(0) == 0)
    def _():
        f = f_ref[0:1, :]
        w_ref[:DS] = (xgt_ref[:DS].astype(F32) * (SCALE * f)).astype(BF16)
        w_ref[DS:] = (xgt_ref[DS:].astype(F32) * f).astype(BF16)

    out_ref[...] = jnp.dot(w_ref[:DS], ds_ref[...], preferred_element_type=F32) + jnp.dot(
        w_ref[DS:], e_ref[...], preferred_element_type=F32
    )


def book_grad(xgt, f, ds, e, first, width, tile=1024):
    rows, codes = e.shape
    pairs = rows * width
    start = first // tile
    return pl.pallas_call(
        book_body,
        grid=(width // tile,),
        in_specs=[
            pl.BlockSpec((LANES, rows), lambda t: (0, 0)),
            pl.BlockSpec((8, rows), lambda t: (0, 0)),
            pl.BlockSpec((rows, tile), lambda t: (0, start + t)),
            pl.BlockSpec((rows, tile), lambda t: (0, start + t)),
        ],
        out_specs=pl.BlockSpec((DS, tile), lambda t: (0, t)),
        out_shape=jax.ShapeDtypeStruct((DS, width), F32),
        scratch_shapes=[pltpu.VMEM((LANES, rows), BF16)],
        compiler_params=pltpu.CompilerParams(vmem_limit_bytes=VMEM_LIMIT),
        cost_estimate=pl.CostEstimate(flops=pairs * 1024, bytes_accessed=pairs * 4, transcendentals=0),
        name="book_grad",
    )(xgt, f, ds, e)


def local(n_sub, n_code, inputs, upstream, codebook):
    n_z = n_code // 2
    place = lax.axis_index("code")
    core, z = place % 2, place // 2
    mine = inputs.shape[0] // 2

    def to_mate(v):
        return lax.ppermute(v, "code", [(j, j ^ 1) for j in range(n_code)])

    def along_z(v, d):
        return lax.ppermute(v, "code", [(j, (j + 2 * d) % n_code) for j in range(n_code)])

    def cut(v):
        return lax.dynamic_slice_in_dim(v, core * mine, mine, 0).reshape(mine, n_sub, DS)

    xg = jnp.concatenate([cut(inputs), cut(upstream)], axis=2).transpose(1, 0, 2)
    xg = lax.all_to_all(xg, "sub", 0, 0, tiled=True).reshape(n_sub * mine, LANES)

    own_book = codebook[0]
    width = own_book.shape[1]
    book = jnp.concatenate([own_book, to_mate(own_book)], axis=1)
    codes = book.shape[1]
    bookt = jnp.concatenate(
        [book.T, jnp.ones((codes, 1), BF16), jnp.zeros((codes, LANES - DS - 1), BF16)], axis=1
    )

    e, part, stat, xgt = scores(xg, book, bookt)
    stats = [stat] + [along_z(stat, d) for d in range(1, n_z)]
    ds, out, f = slopes(xg, book, bookt, e, part, stats)

    out = lax.all_to_all(out, "sub", 0, 0, tiled=True)
    step = mine // n_z
    pieces = out.reshape(n_sub, n_z, step, LANES)
    piece = lambda k: lax.dynamic_index_in_dim(pieces, k, 1, keepdims=False)
    total = piece(z).astype(F32)
    for d in range(1, n_z):
        total = total + along_z(piece((z + d) % n_z), d).astype(F32)
    total = total.astype(BF16)
    ring = [along_z(total, d) for d in range(n_z - 1, 0, -1)] + [total]
    whole = lax.dynamic_slice_in_dim(jnp.stack(ring + ring), n_z - 1 - z, n_z, 0)
    half = whole.reshape(n_z, n_sub, step, 2, DS).transpose(3, 0, 2, 1, 4).reshape(2, mine, n_sub * DS)
    other = to_mate(half)
    both = jnp.concatenate([jnp.where(core == 0, half, other), jnp.where(core == 0, other, half)], axis=1)

    far = book_grad(xgt, f, ds, e, width, width)
    near = book_grad(xgt, f, ds, e, 0, width)
    grad_book = near + to_mate(far)
    return both[0], both[1], grad_book[None]


def solution(mesh):
    in_specs = (P("sub", None), P("sub", None), P("sub", None, "code"))
    out_specs = (P("sub", None), P("sub", None), P("sub", None, "code"))
    body = functools.partial(local, mesh.shape["sub"], mesh.shape["code"])
    return jax.shard_map(body, mesh=mesh, in_specs=in_specs, out_specs=out_specs, check_vma=False)
```

```python
import functools

import jax
import jax.numpy as jnp
from jax import lax
from jax.experimental import pallas as pl
from jax.experimental.pallas import tpu as pltpu
from jax.sharding import PartitionSpec as P

BF16 = jnp.bfloat16
F32 = jnp.float32
DS = 64
LANES = 128
SCALE = 0.25
LOG2E = 1.4426950408889634
MIB = 2**20
WHOLE = pl.BlockSpec(memory_space=pltpu.VMEM)
SCALAR = pl.BlockSpec(memory_space=pltpu.SMEM)


def span(start, size):
    return pl.ds(pl.multiple_of(start, size), size)


def small(body, name, n_in, outs, flops=10**8):
    return pl.pallas_call(
        body,
        in_specs=[SCALAR] + [WHOLE] * n_in,
        out_specs=[WHOLE] * len(outs),
        out_shape=outs,
        compiler_params=pltpu.CompilerParams(vmem_limit_bytes=12 * MIB),
        cost_estimate=pl.CostEstimate(flops=flops, bytes_accessed=2**21, transcendentals=0),
        name=name,
    )


def pack_body(place_ref, x_ref, g_ref, out_ref):
    subs, rows, _ = out_ref.shape
    at = pl.ds(pl.multiple_of(place_ref[0] * rows, rows), rows)
    for k in range(0, subs, 2):
        cols = slice(k * DS, (k + 2) * DS)
        x, g = x_ref[at, cols], g_ref[at, cols]
        out_ref[k] = jnp.concatenate([x[:, :DS], g[:, :DS]], axis=1)
        out_ref[k + 1] = jnp.concatenate([x[:, DS:], g[:, DS:]], axis=1)


def book_body_prep(place_ref, own_ref, mate_ref, book_ref, bookt_ref):
    width = own_ref.shape[1]
    step = 512
    lane = lax.broadcasted_iota(jnp.int32, (step, LANES), 1)
    for n, ref in enumerate((own_ref, mate_ref)):
        book_ref[:, n * width : (n + 1) * width] = ref[...]
        for c in range(0, width, step):
            v = ref[:, c : c + step].astype(F32)
            turned = jnp.concatenate([v, jnp.zeros_like(v)], axis=0).T
            bookt_ref[n * width + c : n * width + c + step, :] = jnp.where(lane == DS, 1.0, turned).astype(BF16)


def local_pass_body(chunk, tiles, xg_ref, book_ref, bookt_ref, e_ref, ds_ref, part_ref, dx_ref, stat_ref, xgt_ref, *scratch):
    s_slots, m_slots, e_slots, gq_slots, d_slots = (scratch[k : k + 2] for k in range(0, 10, 2))
    t = pl.program_id(0)
    tile, codes = e_ref.shape
    steps = codes // chunk

    def look(n):
        x = xg_ref[span(t * tile, tile), :][:, :DS]
        most = None

        def one(c):
            nonlocal most
            if c == steps:
                return
            s = jnp.dot(x, book_ref[:, c * chunk : (c + 1) * chunk], preferred_element_type=F32)
            s_slots[n][:, c * chunk : (c + 1) * chunk] = s
            for k in range(0, chunk, LANES):
                piece = s[:, k : k + LANES]
                most = piece if most is None else jnp.maximum(most, piece)

        def end():
            top = jnp.max(most, axis=1, keepdims=True) * (SCALE * LOG2E)
            m_slots[n][...] = jnp.broadcast_to(top, (tile, LANES))

        return one, end

    def weigh(n):
        top = m_slots[n][...]
        wide = jnp.concatenate([top] * (chunk // LANES), axis=1)
        acc = jnp.zeros((tile, LANES), F32)

        def one(c):
            nonlocal acc
            if c == steps:
                return
            at = slice(c * chunk, (c + 1) * chunk)
            e = jnp.exp2(s_slots[n][:, at] * (SCALE * LOG2E) - wide).astype(BF16)
            e_ref[:, at] = e
            e_slots[n][:, at] = e
            acc = acc + jnp.dot(e, bookt_ref[at, :], preferred_element_type=F32)

        def end():
            part_ref[...] = acc
            lane = lax.broadcasted_iota(jnp.int32, (tile, LANES), 1)
            total = jnp.sum(jnp.where(lane == DS, acc, 0.0), axis=1, keepdims=True)
            xg = xg_ref[span((t - 1) * tile, tile), :]
            h = jnp.sum(acc[:, :DS] * xg[:, DS:].astype(F32), axis=1, keepdims=True)
            gq = h / total
            gq_slots[n][...] = jnp.broadcast_to(gq, (tile, LANES))
            stat = jnp.where(lane == 0, top, jnp.where(lane == 1, total, jnp.where(lane == 2, h, gq)))
            stat_ref[...] = stat.T[:8]
            xgt_ref[...] = xg.T

        return one, end

    def lean(n):
        g = xg_ref[span((t - 2) * tile, tile), :][:, DS:]
        wide = jnp.concatenate([gq_slots[n][...]] * (chunk // LANES), axis=1)
        acc = jnp.zeros((tile, LANES), F32)

        def one(c):
            nonlocal acc
            if c < steps:
                at = slice(c * chunk, (c + 1) * chunk)
                d_slots[c % 2][...] = jnp.dot(g, book_ref[:, at], preferred_element_type=F32) - wide
            if c > 0:
                at = slice((c - 1) * chunk, c * chunk)
                ds = (d_slots[(c - 1) % 2][...] * e_slots[n][:, at].astype(F32)).astype(BF16)
                ds_ref[:, at] = ds
                acc = acc + jnp.dot(ds, bookt_ref[at, :], preferred_element_type=F32)

        def end():
            dx_ref[...] = acc

        return one, end

    def run(*works):
        for c in range(steps + 1):
            for one, _ in works:
                one(c)
        for _, end in works:
            end()

    for n in range(2):
        full = jnp.logical_and(jnp.logical_and(t >= 2, t < tiles), t % 2 == n)

        @pl.when(full)
        def _():
            run(look(n), weigh(1 - n), lean(n))

    last = tiles % 2

    @pl.when(t == 0)
    def _():
        run(look(0))

    @pl.when(t == 1)
    def _():
        run(look(1), weigh(0))

    @pl.when(t == tiles)
    def _():
        run(weigh(1 - last), lean(last))

    @pl.when(t == tiles + 1)
    def _():
        run(lean(1 - last))


def local_pass(xg, book, bookt, tile=128, chunk=1024):
    rows, codes = xg.shape[0], book.shape[1]
    tiles = rows // tile
    pairs = rows * codes
    back = lambda n: lambda t: jnp.clip(t - n, 0, tiles - 1)
    by_row = lambda w, n: pl.BlockSpec((tile, w), lambda t: (back(n)(t), 0))
    by_col = lambda h, n: pl.BlockSpec((h, tile), lambda t: (0, back(n)(t)))
    fixed = lambda *shape: pl.BlockSpec(shape, lambda t: (0, 0))
    wide, narrow = pltpu.VMEM((tile, codes), F32), pltpu.VMEM((tile, LANES), F32)
    return pl.pallas_call(
        functools.partial(local_pass_body, chunk, tiles),
        grid=(tiles + 2,),
        in_specs=[fixed(rows, LANES), fixed(DS, codes), fixed(codes, LANES)],
        out_specs=[by_row(codes, 1), by_row(codes, 2), by_row(LANES, 1), by_row(LANES, 2), by_col(8, 1), by_col(LANES, 1)],
        out_shape=[
            jax.ShapeDtypeStruct((rows, codes), BF16),
            jax.ShapeDtypeStruct((rows, codes), BF16),
            jax.ShapeDtypeStruct((rows, LANES), F32),
            jax.ShapeDtypeStruct((rows, LANES), F32),
            jax.ShapeDtypeStruct((8, rows), F32),
            jax.ShapeDtypeStruct((LANES, rows), BF16),
        ],
        scratch_shapes=[wide, wide, narrow, narrow]
        + [pltpu.VMEM((tile, codes), BF16)] * 2
        + [narrow, narrow]
        + [pltpu.VMEM((tile, chunk), F32)] * 2,
        compiler_params=pltpu.CompilerParams(vmem_limit_bytes=44 * MIB),
        cost_estimate=pl.CostEstimate(flops=pairs * 2048, bytes_accessed=pairs * 4, transcendentals=pairs),
        name="local_pass",
    )(xg, book, bookt)


def mix_body(part_ref, dx_ref, xgt_ref, own_ref, o1, o2, o3, out_ref, w_ref):
    rows = part_ref.shape[0]
    stats = [r[...] for r in (own_ref, o1, o2, o3)]
    top = functools.reduce(jnp.maximum, [s[0:1] for s in stats])
    rel = [jnp.exp2(s[0:1] - top) for s in stats]
    z = sum(r * s[1:2] for r, s in zip(rel, stats))
    gq = sum(r * s[2:3] for r, s in zip(rel, stats)) / z
    f_row = rel[0] / z
    off_row = stats[0][3:4] - gq
    x, g = xgt_ref[:DS].astype(F32), xgt_ref[DS:].astype(F32)
    w_ref[:DS] = (x * (SCALE * f_row)).astype(BF16)
    w_ref[DS:] = ((g + (SCALE * off_row) * x) * f_row).astype(BF16)
    step = LANES
    sub = lax.broadcasted_iota(jnp.int32, (LANES, step), 0)
    for r in range(0, rows, step):
        at = slice(r, r + step)
        turned = jnp.where(sub == 0, f_row[:, at], off_row[:, at]).T
        f, off = turned[:, 0:1], turned[:, 1:2]
        part = part_ref[at, :]
        q = (part * f)[:, :DS]
        dx = ((dx_ref[at, :] + part * off) * (SCALE * f))[:, :DS]
        out_ref[at, :] = jnp.concatenate([q, dx], axis=1).astype(BF16)


def mix(part, dx, xgt, stats):
    rows = part.shape[0]
    return pl.pallas_call(
        mix_body,
        in_specs=[WHOLE] * 7,
        out_specs=[WHOLE] * 2,
        out_shape=[jax.ShapeDtypeStruct((rows, LANES), BF16), jax.ShapeDtypeStruct((LANES, rows), BF16)],
        compiler_params=pltpu.CompilerParams(vmem_limit_bytes=12 * MIB),
        cost_estimate=pl.CostEstimate(flops=10**8, bytes_accessed=2**22, transcendentals=0),
        name="mix",
    )(part, dx, xgt, *stats)


def book_body(w_ref, ds_ref, e_ref, *rest):
    out_ref = rest[-1]
    grad = jnp.dot(w_ref[:DS], ds_ref[...], preferred_element_type=F32)
    grad += jnp.dot(w_ref[DS:], e_ref[...], preferred_element_type=F32)
    if len(rest) > 1:
        grad += rest[0][...]
    out_ref[...] = grad


def book_grad(w, ds, e, first, width, whole, other=None, before=None, tile=1024):
    rows, codes = e.shape
    pairs = rows * width
    start = first // tile
    into = first % whole // tile
    tall = pl.BlockSpec((rows, tile), lambda t: (0, start + t))
    flat = pl.BlockSpec((DS, tile), lambda t: (0, into + t))
    more = [] if other is None else [other]
    kept = [] if before is None else [before]
    return pl.pallas_call(
        book_body,
        grid=(width // tile,),
        in_specs=[pl.BlockSpec((LANES, rows), lambda t: (0, 0)), tall, tall]
        + [flat] * len(more)
        + [pl.BlockSpec(memory_space=pl.ANY)] * len(kept),
        out_specs=flat,
        out_shape=jax.ShapeDtypeStruct((DS, whole), F32),
        input_output_aliases={4: 0} if kept else {},
        compiler_params=pltpu.CompilerParams(vmem_limit_bytes=28 * MIB),
        cost_estimate=pl.CostEstimate(flops=pairs * 1024, bytes_accessed=pairs * 4, transcendentals=0),
        name="book_grad",
    )(w, ds, e, *more, *kept)


def pieces_body(n_z, place_ref, a_ref, own_ref, *send_refs):
    part = own_ref.shape[1]
    for d, out in enumerate((own_ref, *send_refs)):
        out[...] = a_ref[:, span(lax.rem(place_ref[1] + d, n_z) * part, part)]


def sum_body(place_ref, *refs):
    *ins, out = refs
    out[...] = sum(r[...].astype(F32) for r in ins).astype(BF16)


def spread_body(n_z, place_ref, *refs):
    *ins, q_ref, dx_ref = refs
    subs, part, _ = ins[0].shape
    for n, ref in enumerate(ins):
        swap, d = n // n_z, n % n_z
        core = place_ref[0] if swap == 0 else 1 - place_ref[0]
        at = span((core * n_z + lax.rem(place_ref[1] + n_z - d, n_z)) * part, part)
        for k in range(0, subs, 2):
            a, b = ref[k], ref[k + 1]
            cols = slice(k * DS, (k + 2) * DS)
            q_ref[at, cols] = jnp.concatenate([a[:, :DS], b[:, :DS]], axis=1)
            dx_ref[at, cols] = jnp.concatenate([a[:, DS:], b[:, DS:]], axis=1)


def local(n_sub, n_code, inputs, upstream, codebook):
    n_z = n_code // 2
    index = lax.axis_index("code")
    place = jnp.stack([index % 2, index // 2]).astype(jnp.int32)
    n_rows, width_all = inputs.shape
    mine = n_rows // 2
    shaped = jax.ShapeDtypeStruct
    then = lax.optimization_barrier

    def to_peer(v, d, swap=0):
        pairs = [(j, ((j // 2 + d) % n_z) * 2 + (j % 2 ^ swap)) for j in range(n_code)]
        return lax.ppermute(v, "code", pairs)

    own_book = codebook[0]
    width = own_book.shape[1]
    mate_book = to_peer(own_book, 0, 1)
    (xg,) = small(pack_body, "pack", 2, [shaped((n_sub, mine, LANES), BF16)])(place, inputs, upstream)
    xg = lax.all_to_all(xg, "sub", 0, 0, tiled=True)
    book, bookt = small(
        book_body_prep, "books", 2, [shaped((DS, 2 * width), BF16), shaped((2 * width, LANES), BF16)], 10**10
    )(place, own_book, mate_book)

    xg = xg.reshape(n_sub * mine, LANES)
    e, ds, part, dxl, stat, xgt = local_pass(xg, book, bookt)
    stats = [stat] + [to_peer(stat, d) for d in range(1, n_z)]
    out, w = mix(part, dxl, xgt, stats)

    moved = lax.all_to_all(out.reshape(n_sub, mine, LANES), "sub", 0, 0, tiled=True)
    far = book_grad(w, ds, e, width, width, width)
    moved, far = then((moved, far))
    from_far = to_peer(far, 0, 1)
    piece = shaped((n_sub, mine // n_z, LANES), BF16)
    own, *sends = small(functools.partial(pieces_body, n_z), "pieces", 1, [piece] * n_z)(place, moved)
    w, own, sends, from_far = then((w, own, sends, from_far))
    near = book_grad(w, ds, e, 0, width // 2, width, from_far)
    got, near = then(([to_peer(v, d) for d, v in enumerate(sends, 1)], near))
    (total,) = small(sum_body, "sums", n_z, [piece])(place, own, *got)
    w, total = then((w, total))
    near = book_grad(w, ds, e, width // 2, width // 2, width, from_far, near)
    ring = [total] + [to_peer(total, d) for d in range(1, n_z)]
    ring, near = then((ring, near))
    every = ring + [to_peer(v, 0, 1) for v in ring]
    quantized, grads = small(functools.partial(spread_body, n_z), "spread", n_code, [shaped(inputs.shape, BF16)] * 2)(
        place, *every
    )
    return quantized, grads, near[None]


def solution(mesh):
    in_specs = (P("sub", None), P("sub", None), P("sub", None, "code"))
    out_specs = (P("sub", None), P("sub", None), P("sub", None, "code"))
    body = functools.partial(local, mesh.shape["sub"], mesh.shape["code"])
    return jax.shard_map(body, mesh=mesh, in_specs=in_specs, out_specs=out_specs, check_vma=False)
```

```python
import functools

import jax
import jax.numpy as jnp
from jax import lax
from jax.experimental import pallas as pl
from jax.experimental.pallas import tpu as pltpu
from jax.sharding import PartitionSpec as P

BF16 = jnp.bfloat16
F32 = jnp.float32
DS = 64
LANES = 128
SCALE = 0.25
LOG2E = 1.4426950408889634
MIB = 2**20
PASS_MIB = 34
WHOLE = pl.BlockSpec(memory_space=pltpu.VMEM)
FAR = pl.BlockSpec(memory_space=pltpu.HBM)
SCALAR = pl.BlockSpec(memory_space=pltpu.SMEM)


def span(start, size):
    return pl.ds(pl.multiple_of(start, size), size)


def small(body, name, n_in, outs, flops=10**8):
    return pl.pallas_call(
        body,
        in_specs=[SCALAR] + [WHOLE] * n_in,
        out_specs=[WHOLE] * len(outs),
        out_shape=outs,
        compiler_params=pltpu.CompilerParams(vmem_limit_bytes=12 * MIB),
        cost_estimate=pl.CostEstimate(flops=flops, bytes_accessed=2**21, transcendentals=0),
        name=name,
    )


def pack_body(place_ref, x_hbm, g_hbm, out_ref, x_ref, g_ref, sems):
    subs, rows, _ = out_ref.shape
    at = span(place_ref[0] * rows, rows)
    copies = [
        pltpu.make_async_copy(src.at[at], dst, sems.at[k])
        for k, (src, dst) in enumerate(((x_hbm, x_ref), (g_hbm, g_ref)))
    ]
    for copy in copies:
        copy.start()
    for copy in copies:
        copy.wait()
    for k in range(0, subs, 2):
        cols = slice(k * DS, (k + 2) * DS)
        x, g = x_ref[:, cols], g_ref[:, cols]
        out_ref[k] = jnp.concatenate([x[:, :DS], g[:, :DS]], axis=1)
        out_ref[k + 1] = jnp.concatenate([x[:, DS:], g[:, DS:]], axis=1)


def pack(place, x, g, subs):
    rows, width = x.shape[0] // 2, x.shape[1]
    far = lambda v: pltpu.with_memory_space_constraint(v, pltpu.HBM)
    return pl.pallas_call(
        pack_body,
        in_specs=[SCALAR, FAR, FAR],
        out_specs=WHOLE,
        out_shape=jax.ShapeDtypeStruct((subs, rows, LANES), BF16),
        scratch_shapes=[pltpu.VMEM((rows, width), BF16)] * 2 + [pltpu.SemaphoreType.DMA((2,))],
        compiler_params=pltpu.CompilerParams(vmem_limit_bytes=8 * MIB),
        cost_estimate=pl.CostEstimate(flops=10**8, bytes_accessed=2**21, transcendentals=0),
        name="pack",
    )(place, far(x), far(g))


def book_body_prep(place_ref, own_ref, mate_ref, book_ref, bookt_ref):
    width = own_ref.shape[1]
    step = 512
    lane = lax.broadcasted_iota(jnp.int32, (step, LANES), 1)
    for n, ref in enumerate((own_ref, mate_ref)):
        book_ref[:, n * width : (n + 1) * width] = ref[...]
        for c in range(0, width, step):
            v = ref[:, c : c + step].astype(F32)
            turned = jnp.concatenate([v, jnp.zeros_like(v)], axis=0).T
            bookt_ref[n * width + c : n * width + c + step, :] = jnp.where(lane == DS, 1.0, turned).astype(BF16)


def local_pass_body(chunk, parts, xg_ref, book_ref, bookt_ref, *rest):
    e_refs, rest = rest[: len(parts)], rest[len(parts) :]
    ds_hbm, part_ref, dx_ref, stat_ref, xgt_ref, *scratch = rest
    s_slots, m_slots, gq_slots, d_slots, ds_slots, e_slots = (scratch[k : k + 2] for k in range(0, 12, 2))
    e_sems, ds_sems = scratch[12:]
    tile, codes = s_slots[0].shape
    tiles = xg_ref.shape[0] // tile
    steps = codes // chunk
    rows = lambda t: span(t * tile, tile)

    def e_at(t, n, c):
        for ref, (first, width, kept, place) in zip(e_refs, parts):
            at = c * chunk - first
            if 0 <= at < width:
                if kept:
                    return ref, (rows(t), slice(at, at + chunk))
                return e_slots[n], (slice(None), slice(place + at, place + at + chunk))

    def e_copies(t, n):
        return [
            pltpu.make_async_copy(e_slots[n].at[:, place : place + width], ref.at[rows(t)], e_sems.at[n, k])
            for k, (ref, (_, width, kept, place)) in enumerate(zip(e_refs, parts))
            if not kept
        ]

    def ds_copy(t, n):
        return pltpu.make_async_copy(ds_slots[n], ds_hbm.at[rows(t)], ds_sems.at[n])

    def look(t, n):
        x = xg_ref[rows(t), :][:, :DS]
        most = None

        def one(c):
            nonlocal most
            if c == steps:
                return
            s = jnp.dot(x, book_ref[:, c * chunk : (c + 1) * chunk], preferred_element_type=F32)
            s_slots[n][:, c * chunk : (c + 1) * chunk] = s
            for k in range(0, chunk, LANES):
                piece = s[:, k : k + LANES]
                most = piece if most is None else jnp.maximum(most, piece)

        def end():
            top = jnp.max(most, axis=1, keepdims=True) * (SCALE * LOG2E)
            m_slots[n][...] = jnp.broadcast_to(top, (tile, LANES))

        return one, end

    def weigh(t, n):
        top = m_slots[n][...]
        wide = jnp.concatenate([top] * (chunk // LANES), axis=1)
        acc = jnp.zeros((tile, LANES), F32)

        def one(c):
            nonlocal acc
            if c == steps:
                return
            at = slice(c * chunk, (c + 1) * chunk)
            e = jnp.exp2(s_slots[n][:, at] * (SCALE * LOG2E) - wide).astype(BF16)
            ref, place = e_at(t, n, c)
            ref[place] = e
            acc = acc + jnp.dot(e, bookt_ref[at, :], preferred_element_type=F32)

        def end():
            part_ref[rows(t), :] = acc
            lane = lax.broadcasted_iota(jnp.int32, (tile, LANES), 1)
            total = jnp.sum(jnp.where(lane == DS, acc, 0.0), axis=1, keepdims=True)
            xg = xg_ref[rows(t), :]
            h = jnp.sum(acc[:, :DS] * xg[:, DS:].astype(F32), axis=1, keepdims=True)
            gq = h / total
            gq_slots[n][...] = jnp.broadcast_to(gq, (tile, LANES))
            stat = jnp.where(lane == 0, top, jnp.where(lane == 1, total, jnp.where(lane == 2, h, gq)))
            stat_ref[:, rows(t)] = stat.T[:8]
            xgt_ref[:, rows(t)] = xg.T
            for copy in e_copies(t, n):
                copy.start()

        return one, end

    def lean(t, n):
        g = xg_ref[rows(t), :][:, DS:]
        wide = jnp.concatenate([gq_slots[n][...]] * (chunk // LANES), axis=1)
        acc = jnp.zeros((tile, LANES), F32)

        def one(c):
            nonlocal acc
            if c < steps:
                at = slice(c * chunk, (c + 1) * chunk)
                d_slots[c % 2][...] = jnp.dot(g, book_ref[:, at], preferred_element_type=F32) - wide
            if c > 0:
                at = slice((c - 1) * chunk, c * chunk)
                ref, place = e_at(t, n, c - 1)
                ds = (d_slots[(c - 1) % 2][...] * ref[place].astype(F32)).astype(BF16)
                ds_slots[n][:, at] = ds
                acc = acc + jnp.dot(ds, bookt_ref[at, :], preferred_element_type=F32)

        def end():
            dx_ref[rows(t), :] = acc
            ds_copy(t, n).start()

        return one, end

    def wait_e(t, n):
        for copy in e_copies(t, n):
            copy.wait()

    def run(*works):
        for c in range(steps + 1):
            for one, _ in works:
                one(c)
        for _, end in works:
            end()

    run(look(0, 0))
    run(look(1, 1), weigh(0, 0))

    def two(i, carry):
        for n in range(2):
            t = 2 + 2 * i + n
            if n == 0:

                @pl.when(i > 0)
                def _():
                    wait_e(t - 3, 1)
                    ds_copy(t - 4, 0).wait()

            else:
                wait_e(t - 3, 0)

                @pl.when(i > 0)
                def _():
                    ds_copy(t - 4, 1).wait()

            run(look(t, n), weigh(t - 1, 1 - n), lean(t - 2, n))
        return carry

    lax.fori_loop(0, tiles // 2 - 1, two, 0)
    wait_e(tiles - 3, 1)
    ds_copy(tiles - 4, 0).wait()
    run(weigh(tiles - 1, 1), lean(tiles - 2, 0))
    ds_copy(tiles - 3, 1).wait()
    run(lean(tiles - 1, 1))
    wait_e(tiles - 2, 0)
    wait_e(tiles - 1, 1)
    ds_copy(tiles - 2, 0).wait()
    ds_copy(tiles - 1, 1).wait()


def local_pass(xg, book, bookt, parts, tile=128, chunk=1024):
    rows, codes = xg.shape[0], book.shape[1]
    pairs = rows * codes
    staged, placed = 0, []
    for first, width, kept in parts:
        placed.append((first, width, kept, staged))
        staged += 0 if kept else width
    wide, narrow, short = pltpu.VMEM((tile, codes), F32), pltpu.VMEM((tile, LANES), F32), pltpu.VMEM((tile, codes), BF16)
    return pl.pallas_call(
        functools.partial(local_pass_body, chunk, tuple(placed)),
        in_specs=[WHOLE] * 3,
        out_specs=[WHOLE if kept else FAR for _, _, kept in parts] + [FAR] + [WHOLE] * 4,
        out_shape=[(pltpu.VMEM if kept else pltpu.HBM)((rows, width), BF16) for _, width, kept in parts]
        + [
            pltpu.HBM((rows, codes), BF16),
            jax.ShapeDtypeStruct((rows, LANES), F32),
            jax.ShapeDtypeStruct((rows, LANES), F32),
            jax.ShapeDtypeStruct((8, rows), F32),
            jax.ShapeDtypeStruct((LANES, rows), BF16),
        ],
        scratch_shapes=[wide, wide, narrow, narrow, narrow, narrow]
        + [pltpu.VMEM((tile, chunk), F32)] * 2
        + [short, short]
        + [pltpu.VMEM((tile, max(staged, LANES)), BF16)] * 2
        + [pltpu.SemaphoreType.DMA((2, len(parts))), pltpu.SemaphoreType.DMA((2,))],
        compiler_params=pltpu.CompilerParams(vmem_limit_bytes=PASS_MIB * MIB),
        cost_estimate=pl.CostEstimate(flops=pairs * 2048, bytes_accessed=pairs * 4, transcendentals=pairs),
        name="local_pass",
    )(xg, book, bookt)


def mix_body(part_ref, dx_ref, xgt_ref, own_ref, o1, o2, o3, out_ref, w_ref):
    rows = part_ref.shape[0]
    stats = [r[...] for r in (own_ref, o1, o2, o3)]
    top = functools.reduce(jnp.maximum, [s[0:1] for s in stats])
    rel = [jnp.exp2(s[0:1] - top) for s in stats]
    z = sum(r * s[1:2] for r, s in zip(rel, stats))
    gq = sum(r * s[2:3] for r, s in zip(rel, stats)) / z
    f_row = rel[0] / z
    off_row = stats[0][3:4] - gq
    x, g = xgt_ref[:DS].astype(F32), xgt_ref[DS:].astype(F32)
    w_ref[:DS] = (x * (SCALE * f_row)).astype(BF16)
    w_ref[DS:] = ((g + (SCALE * off_row) * x) * f_row).astype(BF16)
    step = LANES
    sub = lax.broadcasted_iota(jnp.int32, (8, step), 0)
    for r in range(0, rows, step):
        at = slice(r, r + step)
        turned = jnp.where(sub == 0, f_row[:, at], off_row[:, at]).T
        f, off = turned[:, 0:1], turned[:, 1:2]
        part = part_ref[at, :]
        q = (part * f)[:, :DS]
        dx = ((dx_ref[at, :] + part * off) * (SCALE * f))[:, :DS]
        out_ref[at, :] = jnp.concatenate([q, dx], axis=1).astype(BF16)


def mix(part, dx, xgt, stats):
    rows = part.shape[0]
    return pl.pallas_call(
        mix_body,
        in_specs=[WHOLE] * 7,
        out_specs=[WHOLE] * 2,
        out_shape=[jax.ShapeDtypeStruct((rows, LANES), BF16), jax.ShapeDtypeStruct((LANES, rows), BF16)],
        compiler_params=pltpu.CompilerParams(vmem_limit_bytes=12 * MIB),
        cost_estimate=pl.CostEstimate(flops=10**8, bytes_accessed=2**22, transcendentals=0),
        name="mix",
    )(part, dx, xgt, *stats)


def book_body(first, tile, kept, extra, w_ref, ds_hbm, e_ref, *rest):
    out_ref = rest[extra]

    def one(ds_ref, *more):
        at = span(pl.program_id(0) * tile, tile)
        e = e_ref[:, at] if kept else more[0][...]
        grad = jnp.dot(w_ref[:DS], ds_ref[...], preferred_element_type=F32)
        grad += jnp.dot(w_ref[DS:], e, preferred_element_type=F32)
        if extra:
            grad += rest[0][:, at]
        out_ref[:, at] = grad

    rows, width = e_ref.shape
    specs = [pl.BlockSpec((rows, tile), lambda t: (0, first // tile + t))]
    if not kept:
        specs.append(pl.BlockSpec((rows, tile), lambda t: (0, t)))
    pltpu.emit_pipeline(one, grid=(width // tile,), in_specs=specs)(ds_hbm, *([] if kept else [e_ref]))


def book_grad(w, ds, e, part, other=None):
    first, width, kept = part
    tile = 1024 if width > 2048 else 512
    rows = e.shape[0]
    pairs = rows * width
    more = [] if other is None else [other]
    space = pltpu.VMEM if kept else pltpu.HBM
    return pl.pallas_call(
        functools.partial(book_body, first, tile, kept, len(more)),
        in_specs=[WHOLE, FAR, WHOLE if kept else FAR] + [WHOLE] * len(more),
        out_specs=WHOLE,
        out_shape=jax.ShapeDtypeStruct((DS, width), F32),
        compiler_params=pltpu.CompilerParams(vmem_limit_bytes=(14 if kept else 24) * MIB),
        cost_estimate=pl.CostEstimate(flops=pairs * 1024, bytes_accessed=pairs * 4, transcendentals=0),
        name="book_grad",
    )(w, pltpu.with_memory_space_constraint(ds, pltpu.HBM), pltpu.with_memory_space_constraint(e, space), *more)


def pieces_body(n_z, place_ref, a_ref, own_ref, *send_refs):
    part = own_ref.shape[1]
    for d, out in enumerate((own_ref, *send_refs)):
        out[...] = a_ref[:, span(lax.rem(place_ref[1] + d, n_z) * part, part)]


def sum_body(place_ref, *refs):
    *ins, out = refs
    out[...] = sum(r[...].astype(F32) for r in ins).astype(BF16)


def spread_body(n_z, place_ref, near_1, near_2, from_far, *refs):
    *ins, q_ref, dx_ref, book_ref = refs
    width = near_1.shape[1]
    book_ref[:, :width] = near_1[...] + from_far[:, :width]
    book_ref[:, width:] = near_2[...] + from_far[:, width:]
    subs, part, _ = ins[0].shape
    for n, ref in enumerate(ins):
        swap, d = n // n_z, n % n_z
        core = place_ref[0] if swap == 0 else 1 - place_ref[0]
        at = span((core * n_z + lax.rem(place_ref[1] + n_z - d, n_z)) * part, part)
        for k in range(0, subs, 2):
            a, b = ref[k], ref[k + 1]
            cols = slice(k * DS, (k + 2) * DS)
            q_ref[at, cols] = jnp.concatenate([a[:, :DS], b[:, :DS]], axis=1)
            dx_ref[at, cols] = jnp.concatenate([a[:, DS:], b[:, DS:]], axis=1)


def local(n_sub, n_code, inputs, upstream, codebook):
    n_z = n_code // 2
    index = lax.axis_index("code")
    place = jnp.stack([index % 2, index // 2]).astype(jnp.int32)
    n_rows, width_all = inputs.shape
    mine = n_rows // 2
    shaped = jax.ShapeDtypeStruct
    then = lax.optimization_barrier

    def to_peer(v, d, swap=0):
        pairs = [(j, ((j // 2 + d) % n_z) * 2 + (j % 2 ^ swap)) for j in range(n_code)]
        return lax.ppermute(v, "code", pairs)

    own_book = codebook[0]
    width = own_book.shape[1]
    mate_book = to_peer(own_book, 0, 1)
    xg = pack(place, inputs, upstream, n_sub)
    xg = lax.all_to_all(xg, "sub", 0, 0, tiled=True)
    book, bookt = small(
        book_body_prep, "books", 2, [shaped((DS, 2 * width), BF16), shaped((2 * width, LANES), BF16)], 10**10
    )(place, own_book, mate_book)

    xg = xg.reshape(n_sub * mine, LANES)
    parts = [(width, width, False), (0, width // 2, False), (width // 2, width // 2, False)]
    *es, ds, part, dxl, stat, xgt = local_pass(xg, book, bookt, parts)
    stats = [stat] + [to_peer(stat, d) for d in range(1, n_z)]
    out, w = mix(part, dxl, xgt, stats)

    moved = lax.all_to_all(out.reshape(n_sub, mine, LANES), "sub", 0, 0, tiled=True)
    far = book_grad(w, ds, es[0], parts[0])
    moved, far = then((moved, far))
    from_far = to_peer(far, 0, 1)
    piece = shaped((n_sub, mine // n_z, LANES), BF16)
    own, *sends = small(functools.partial(pieces_body, n_z), "pieces", 1, [piece] * n_z)(place, moved)
    w, own, sends = then((w, own, sends))
    near_1 = book_grad(w, ds, es[1], parts[1])
    got, near_1 = then(([to_peer(v, d) for d, v in enumerate(sends, 1)], near_1))
    (total,) = small(sum_body, "sums", n_z, [piece])(place, own, *got)
    w, total = then((w, total))
    near_2 = book_grad(w, ds, es[2], parts[2])
    ring = [total] + [to_peer(total, d) for d in range(1, n_z)]
    ring, near_2 = then((ring, near_2))
    every = ring + [to_peer(v, 0, 1) for v in ring]
    quantized, grads, grad_book = small(
        functools.partial(spread_body, n_z),
        "spread",
        n_code + 3,
        [shaped(inputs.shape, BF16)] * 2 + [shaped((DS, width), F32)],
    )(place, near_1, near_2, from_far, *every)
    return quantized, grads, grad_book[None]


def solution(mesh):
    in_specs = (P("sub", None), P("sub", None), P("sub", None, "code"))
    out_specs = (P("sub", None), P("sub", None), P("sub", None, "code"))
    body = functools.partial(local, mesh.shape["sub"], mesh.shape["code"])
    return jax.shard_map(body, mesh=mesh, in_specs=in_specs, out_specs=out_specs, check_vma=False)
```

```python
import functools

import jax
import jax.numpy as jnp
from jax import lax
from jax.experimental import pallas as pl
from jax.experimental.pallas import tpu as pltpu
from jax.sharding import PartitionSpec as P

BF16 = jnp.bfloat16
F32 = jnp.float32
DS = 64
LANES = 128
SCALE = 0.25
LOG2E = 1.4426950408889634
MIB = 2**20
PASS_MIB = 34
WHOLE = pl.BlockSpec(memory_space=pltpu.VMEM)
FAR = pl.BlockSpec(memory_space=pltpu.HBM)
SCALAR = pl.BlockSpec(memory_space=pltpu.SMEM)


def span(start, size):
    return pl.ds(pl.multiple_of(start, size), size)


def small(body, name, n_in, outs, flops=10**8):
    return pl.pallas_call(
        body,
        in_specs=[SCALAR] + [WHOLE] * n_in,
        out_specs=[WHOLE] * len(outs),
        out_shape=outs,
        compiler_params=pltpu.CompilerParams(vmem_limit_bytes=12 * MIB),
        cost_estimate=pl.CostEstimate(flops=flops, bytes_accessed=2**21, transcendentals=0),
        name=name,
    )


def pack_body(place_ref, x_hbm, g_hbm, out_ref, x_ref, g_ref, sems):
    subs, rows, _ = out_ref.shape
    at = span(place_ref[0] * rows, rows)
    copies = [
        pltpu.make_async_copy(src.at[at], dst, sems.at[k])
        for k, (src, dst) in enumerate(((x_hbm, x_ref), (g_hbm, g_ref)))
    ]
    for copy in copies:
        copy.start()
    for copy in copies:
        copy.wait()
    for k in range(0, subs, 2):
        cols = slice(k * DS, (k + 2) * DS)
        x, g = x_ref[:, cols], g_ref[:, cols]
        out_ref[k] = jnp.concatenate([x[:, :DS], g[:, :DS]], axis=1)
        out_ref[k + 1] = jnp.concatenate([x[:, DS:], g[:, DS:]], axis=1)


def pack(place, x, g, subs):
    rows, width = x.shape[0] // 2, x.shape[1]
    far = lambda v: pltpu.with_memory_space_constraint(v, pltpu.HBM)
    return pl.pallas_call(
        pack_body,
        in_specs=[SCALAR, FAR, FAR],
        out_specs=WHOLE,
        out_shape=jax.ShapeDtypeStruct((subs, rows, LANES), BF16),
        scratch_shapes=[pltpu.VMEM((rows, width), BF16)] * 2 + [pltpu.SemaphoreType.DMA((2,))],
        compiler_params=pltpu.CompilerParams(vmem_limit_bytes=8 * MIB),
        cost_estimate=pl.CostEstimate(flops=10**8, bytes_accessed=2**21, transcendentals=0),
        name="pack",
    )(place, far(x), far(g))


def book_body_prep(place_ref, own_ref, mate_ref, book_ref, bookt_ref):
    width = own_ref.shape[1]
    step = 512
    lane = lax.broadcasted_iota(jnp.int32, (step, LANES), 1)
    for n, ref in enumerate((own_ref, mate_ref)):
        book_ref[:, n * width : (n + 1) * width] = ref[...]
        for c in range(0, width, step):
            v = ref[:, c : c + step].astype(F32)
            turned = jnp.concatenate([v, jnp.zeros_like(v)], axis=0).T
            bookt_ref[n * width + c : n * width + c + step, :] = jnp.where(lane == DS, 1.0, turned).astype(BF16)


def local_pass_body(chunk, parts, xg_ref, book_ref, bookt_ref, *rest):
    e_refs, rest = rest[: len(parts)], rest[len(parts) :]
    ds_hbm, part_ref, dx_ref, stat_ref, xgt_ref, *scratch = rest
    s_slots, m_slots, top_slots, sum_slots, d_slots, ds_slots, e_slots = (scratch[k : k + 2] for k in range(0, 14, 2))
    e_sems, ds_sems = scratch[14:]
    tile, codes = s_slots[0].shape
    tiles = xg_ref.shape[0] // tile
    steps = codes // chunk
    rows = lambda t: span(t * tile, tile)

    def e_at(t, n, c):
        for ref, (first, width, kept, place) in zip(e_refs, parts):
            at = c * chunk - first
            if 0 <= at < width:
                if kept:
                    return ref, (rows(t), slice(at, at + chunk))
                return e_slots[n], (slice(None), slice(place + at, place + at + chunk))

    def e_copies(t, n):
        return [
            pltpu.make_async_copy(e_slots[n].at[:, place : place + width], ref.at[rows(t)], e_sems.at[n, k])
            for k, (ref, (_, width, kept, place)) in enumerate(zip(e_refs, parts))
            if not kept
        ]

    def ds_copy(t, n):
        return pltpu.make_async_copy(ds_slots[n], ds_hbm.at[rows(t)], ds_sems.at[n])

    def look(t, n):
        x = xg_ref[rows(t), :][:, :DS]
        most = None

        def one(c):
            nonlocal most
            if c == steps:
                return
            s = jnp.dot(x, book_ref[:, c * chunk : (c + 1) * chunk], preferred_element_type=F32)
            s_slots[n][:, c * chunk : (c + 1) * chunk] = s
            for k in range(0, chunk, LANES):
                piece = s[:, k : k + LANES]
                most = piece if most is None else jnp.maximum(most, piece)

        def end():
            m_slots[n][...] = most

        return one, end

    def weigh(t, n):
        top = jnp.max(m_slots[n][...], axis=1, keepdims=True) * (SCALE * LOG2E)
        top = jnp.broadcast_to(top, (tile, LANES))
        wide = jnp.concatenate([top] * (chunk // LANES), axis=1)
        acc = jnp.zeros((tile, LANES), F32)

        def one(c):
            nonlocal acc
            if c == steps:
                return
            at = slice(c * chunk, (c + 1) * chunk)
            e = jnp.exp2(s_slots[n][:, at] * (SCALE * LOG2E) - wide).astype(BF16)
            ref, place = e_at(t, n, c)
            ref[place] = e
            acc = acc + jnp.dot(e, bookt_ref[at, :], preferred_element_type=F32)

        def end():
            sum_slots[n][...] = acc
            top_slots[n][...] = top
            for copy in e_copies(t, n):
                copy.start()

        return one, end

    def lean(t, n):
        xg = xg_ref[rows(t), :]
        g = xg[:, DS:]
        sums = sum_slots[n][...]
        lane = lax.broadcasted_iota(jnp.int32, (tile, LANES), 1)
        total = jnp.sum(jnp.where(lane == DS, sums, 0.0), axis=1, keepdims=True)
        h = jnp.sum(sums[:, :DS] * g.astype(F32), axis=1, keepdims=True)
        gq = jnp.broadcast_to(h / total, (tile, LANES))
        wide = jnp.concatenate([gq] * (chunk // LANES), axis=1)
        acc = jnp.zeros((tile, LANES), F32)

        def one(c):
            nonlocal acc
            if c < steps:
                at = slice(c * chunk, (c + 1) * chunk)
                d_slots[c % 2][...] = jnp.dot(g, book_ref[:, at], preferred_element_type=F32) - wide
            if c == 2:
                stat = jnp.where(lane == 0, top_slots[n][...], jnp.where(lane == 1, total, jnp.where(lane == 2, h, gq)))
                stat_ref[:, rows(t)] = stat.T[:8]
                xgt_ref[:, rows(t)] = xg.T
                part_ref[rows(t), :] = jnp.concatenate([sums[:, :DS]] * 2, axis=1)
            if c > 0:
                at = slice((c - 1) * chunk, c * chunk)
                ref, place = e_at(t, n, c - 1)
                ds = (d_slots[(c - 1) % 2][...] * ref[place].astype(F32)).astype(BF16)
                ds_slots[n][:, at] = ds
                acc = acc + jnp.dot(ds, bookt_ref[at, :], preferred_element_type=F32)

        def end():
            dx_ref[rows(t), :] = acc
            ds_copy(t, n).start()

        return one, end

    def wait_e(t, n):
        for copy in e_copies(t, n):
            copy.wait()

    def run(*works):
        for c in range(steps + 1):
            for one, _ in works:
                one(c)
        for _, end in works:
            end()

    run(look(0, 0))
    run(look(1, 1), weigh(0, 0))

    def two(i, carry):
        for n in range(2):
            t = 2 + 2 * i + n
            if n == 0:

                @pl.when(i > 0)
                def _():
                    wait_e(t - 3, 1)
                    ds_copy(t - 4, 0).wait()

            else:
                wait_e(t - 3, 0)

                @pl.when(i > 0)
                def _():
                    ds_copy(t - 4, 1).wait()

            run(look(t, n), weigh(t - 1, 1 - n), lean(t - 2, n))
        return carry

    lax.fori_loop(0, tiles // 2 - 1, two, 0)
    wait_e(tiles - 3, 1)
    ds_copy(tiles - 4, 0).wait()
    run(weigh(tiles - 1, 1), lean(tiles - 2, 0))
    ds_copy(tiles - 3, 1).wait()
    run(lean(tiles - 1, 1))
    wait_e(tiles - 2, 0)
    wait_e(tiles - 1, 1)
    ds_copy(tiles - 2, 0).wait()
    ds_copy(tiles - 1, 1).wait()


def local_pass(xg, book, bookt, parts, tile=128, chunk=1024):
    rows, codes = xg.shape[0], book.shape[1]
    pairs = rows * codes
    staged, placed = 0, []
    for first, width, kept in parts:
        placed.append((first, width, kept, staged))
        staged += 0 if kept else width
    wide, narrow, short = pltpu.VMEM((tile, codes), F32), pltpu.VMEM((tile, LANES), F32), pltpu.VMEM((tile, codes), BF16)
    return pl.pallas_call(
        functools.partial(local_pass_body, chunk, tuple(placed)),
        in_specs=[WHOLE] * 3,
        out_specs=[WHOLE if kept else FAR for _, _, kept in parts] + [FAR] + [WHOLE] * 4,
        out_shape=[(pltpu.VMEM if kept else pltpu.HBM)((rows, width), BF16) for _, width, kept in parts]
        + [
            pltpu.HBM((rows, codes), BF16),
            jax.ShapeDtypeStruct((rows, LANES), F32),
            jax.ShapeDtypeStruct((rows, LANES), F32),
            jax.ShapeDtypeStruct((8, rows), F32),
            jax.ShapeDtypeStruct((LANES, rows), BF16),
        ],
        scratch_shapes=[wide, wide] + [narrow] * 6
        + [pltpu.VMEM((tile, chunk), F32)] * 2
        + [short, short]
        + [pltpu.VMEM((tile, max(staged, LANES)), BF16)] * 2
        + [pltpu.SemaphoreType.DMA((2, len(parts))), pltpu.SemaphoreType.DMA((2,))],
        compiler_params=pltpu.CompilerParams(vmem_limit_bytes=PASS_MIB * MIB),
        cost_estimate=pl.CostEstimate(flops=pairs * 2048, bytes_accessed=pairs * 4, transcendentals=pairs),
        name="local_pass",
    )(xg, book, bookt)


def mix_body(part_ref, dx_ref, xgt_ref, own_ref, o1, o2, o3, out_ref, w_ref):
    rows = part_ref.shape[0]
    stats = [r[...] for r in (own_ref, o1, o2, o3)]
    top = functools.reduce(jnp.maximum, [s[0:1] for s in stats])
    rel = [jnp.exp2(s[0:1] - top) for s in stats]
    z = sum(r * s[1:2] for r, s in zip(rel, stats))
    gq = sum(r * s[2:3] for r, s in zip(rel, stats)) / z
    f_row = rel[0] / z
    off_row = stats[0][3:4] - gq
    x, g = xgt_ref[:DS].astype(F32), xgt_ref[DS:].astype(F32)
    w_ref[:DS] = (x * (SCALE * f_row)).astype(BF16)
    w_ref[DS:] = ((g + (SCALE * off_row) * x) * f_row).astype(BF16)
    step = LANES
    sub = lax.broadcasted_iota(jnp.int32, (8, step), 0)
    lane = lax.broadcasted_iota(jnp.int32, (step, LANES), 1)
    for r in range(0, rows, step):
        at = slice(r, r + step)
        turned = jnp.where(sub == 0, f_row[:, at], off_row[:, at]).T
        f, off = turned[:, 0:1], turned[:, 1:2]
        part = part_ref[at, :]
        dx = dx_ref[at, :][:, :DS]
        lean = (jnp.concatenate([dx, dx], axis=1) + part * off) * SCALE
        out_ref[at, :] = (jnp.where(lane < DS, part, lean) * f).astype(BF16)


def mix(part, dx, xgt, stats):
    rows = part.shape[0]
    return pl.pallas_call(
        mix_body,
        in_specs=[WHOLE] * 7,
        out_specs=[WHOLE] * 2,
        out_shape=[jax.ShapeDtypeStruct((rows, LANES), BF16), jax.ShapeDtypeStruct((LANES, rows), BF16)],
        compiler_params=pltpu.CompilerParams(vmem_limit_bytes=12 * MIB),
        cost_estimate=pl.CostEstimate(flops=10**8, bytes_accessed=2**22, transcendentals=0),
        name="mix",
    )(part, dx, xgt, *stats)


def book_body(first, tile, cuts, w_ref, ds_hbm, e_hbm, out_ref):
    rows, width = e_hbm.shape
    chunk = rows // cuts

    def one(ds_ref, e_ref):
        t, r = pl.program_id(0), pl.program_id(1)
        at = span(t * tile, tile)
        w = w_ref[:, span(r * chunk, chunk)]
        grad = jnp.dot(w[:DS], ds_ref[...], preferred_element_type=F32)
        grad += jnp.dot(w[DS:], e_ref[...], preferred_element_type=F32)
        if cuts == 1:
            out_ref[:, at] = grad
            return

        @pl.when(r == 0)
        def _():
            out_ref[:, at] = grad

        @pl.when(r > 0)
        def _():
            out_ref[:, at] += grad

    specs = [
        pl.BlockSpec((chunk, tile), lambda t, r: (r, first // tile + t)),
        pl.BlockSpec((chunk, tile), lambda t, r: (r, t)),
    ]
    pltpu.emit_pipeline(one, grid=(width // tile, cuts), in_specs=specs)(ds_hbm, e_hbm)


def book_grad(w, ds, e, part):
    first, width, _ = part
    pairs = e.shape[0] * width
    far = lambda v: pltpu.with_memory_space_constraint(v, pltpu.HBM)
    tile, cuts = (1024, 1) if width > 2048 else (512, 1)
    return pl.pallas_call(
        functools.partial(book_body, first, tile, cuts),
        in_specs=[WHOLE, FAR, FAR],
        out_specs=WHOLE,
        out_shape=jax.ShapeDtypeStruct((DS, width), F32),
        compiler_params=pltpu.CompilerParams(vmem_limit_bytes=24 * MIB),
        cost_estimate=pl.CostEstimate(flops=pairs * 1024, bytes_accessed=pairs * 4, transcendentals=0),
        name="book_grad",
    )(w, far(ds), far(e))


def pieces_body(n_z, place_ref, a_ref, own_ref, *send_refs):
    part = own_ref.shape[1]
    for d, out in enumerate((own_ref, *send_refs)):
        out[...] = a_ref[:, span(lax.rem(place_ref[1] + d, n_z) * part, part)]


def sum_body(place_ref, *refs):
    *ins, out = refs
    out[...] = sum(r[...].astype(F32) for r in ins).astype(BF16)


def spread_body(n_z, place_ref, near_1, near_2, from_far, *refs):
    *ins, q_ref, dx_ref, book_ref = refs
    width = near_1.shape[1]
    book_ref[:, :width] = near_1[...] + from_far[:, :width]
    book_ref[:, width:] = near_2[...] + from_far[:, width:]
    subs, part, _ = ins[0].shape
    for n, ref in enumerate(ins):
        swap, d = n // n_z, n % n_z
        core = place_ref[0] if swap == 0 else 1 - place_ref[0]
        at = span((core * n_z + lax.rem(place_ref[1] + n_z - d, n_z)) * part, part)
        for k in range(0, subs, 2):
            a, b = ref[k], ref[k + 1]
            cols = slice(k * DS, (k + 2) * DS)
            q_ref[at, cols] = jnp.concatenate([a[:, :DS], b[:, :DS]], axis=1)
            dx_ref[at, cols] = jnp.concatenate([a[:, DS:], b[:, DS:]], axis=1)


def local(n_sub, n_code, inputs, upstream, codebook):
    n_z = n_code // 2
    index = lax.axis_index("code")
    place = jnp.stack([index % 2, index // 2]).astype(jnp.int32)
    n_rows, width_all = inputs.shape
    mine = n_rows // 2
    shaped = jax.ShapeDtypeStruct
    then = lax.optimization_barrier

    def to_peer(v, d, swap=0):
        pairs = [(j, ((j // 2 + d) % n_z) * 2 + (j % 2 ^ swap)) for j in range(n_code)]
        return lax.ppermute(v, "code", pairs)

    own_book = codebook[0]
    width = own_book.shape[1]
    mate_book = to_peer(own_book, 0, 1)
    xg = pack(place, inputs, upstream, n_sub)
    xg = lax.all_to_all(xg, "sub", 0, 0, tiled=True)
    book, bookt = small(
        book_body_prep, "books", 2, [shaped((DS, 2 * width), BF16), shaped((2 * width, LANES), BF16)], 10**10
    )(place, own_book, mate_book)

    xg = xg.reshape(n_sub * mine, LANES)
    parts = [(width, width, False), (0, width // 2, False), (width // 2, width // 2, False)]
    *es, ds, part, dxl, stat, xgt = local_pass(xg, book, bookt, parts)
    stats = [stat] + [to_peer(stat, d) for d in range(1, n_z)]
    out, w = mix(part, dxl, xgt, stats)

    moved = lax.all_to_all(out.reshape(n_sub, mine, LANES), "sub", 0, 0, tiled=True)
    far = book_grad(w, ds, es[0], parts[0])
    moved, far = then((moved, far))
    from_far = to_peer(far, 0, 1)
    piece = shaped((n_sub, mine // n_z, LANES), BF16)
    own, *sends = small(functools.partial(pieces_body, n_z), "pieces", 1, [piece] * n_z)(place, moved)
    w, own, sends = then((w, own, sends))
    near_1 = book_grad(w, ds, es[1], parts[1])
    got, near_1 = then(([to_peer(v, d) for d, v in enumerate(sends, 1)], near_1))
    (total,) = small(sum_body, "sums", n_z, [piece])(place, own, *got)
    w, total = then((w, total))
    near_2 = book_grad(w, ds, es[2], parts[2])
    ring = [total] + [to_peer(total, d) for d in range(1, n_z)]
    mate_total = to_peer(total, 0, 1)
    ring, mate_total, near_2 = then((ring, mate_total, near_2))
    every = ring + [mate_total] + [to_peer(v, 0, 1) for v in ring[1:]]
    quantized, grads, grad_book = small(
        functools.partial(spread_body, n_z),
        "spread",
        n_code + 3,
        [shaped(inputs.shape, BF16)] * 2 + [shaped((DS, width), F32)],
    )(place, near_1, near_2, from_far, *every)
    return quantized, grads, grad_book[None]


def solution(mesh):
    in_specs = (P("sub", None), P("sub", None), P("sub", None, "code"))
    out_specs = (P("sub", None), P("sub", None), P("sub", None, "code"))
    body = functools.partial(local, mesh.shape["sub"], mesh.shape["code"])
    return jax.shard_map(body, mesh=mesh, in_specs=in_specs, out_specs=out_specs, check_vma=False)
```

```python
import functools

import jax
import jax.numpy as jnp
from jax import lax
from jax.experimental import pallas as pl
from jax.experimental.pallas import tpu as pltpu
from jax.sharding import PartitionSpec as P

BF16 = jnp.bfloat16
F32 = jnp.float32
DS = 64
LANES = 128
SCALE = 0.25
LOG2E = 1.4426950408889634
MIB = 2**20
PASS_MIB = 34
WHOLE = pl.BlockSpec(memory_space=pltpu.VMEM)
FAR = pl.BlockSpec(memory_space=pltpu.HBM)
SCALAR = pl.BlockSpec(memory_space=pltpu.SMEM)


def span(start, size):
    return pl.ds(pl.multiple_of(start, size), size)


def small(body, name, n_in, outs, flops=10**8):
    return pl.pallas_call(
        body,
        in_specs=[SCALAR] + [WHOLE] * n_in,
        out_specs=[WHOLE] * len(outs),
        out_shape=outs,
        compiler_params=pltpu.CompilerParams(vmem_limit_bytes=12 * MIB),
        cost_estimate=pl.CostEstimate(flops=flops, bytes_accessed=2**21, transcendentals=0),
        name=name,
    )


def pack_body(place_ref, x_hbm, g_hbm, out_ref, x_ref, g_ref, sems):
    subs, rows, _ = out_ref.shape
    at = span(place_ref[0] * rows, rows)
    copies = [
        pltpu.make_async_copy(src.at[at], dst, sems.at[k])
        for k, (src, dst) in enumerate(((x_hbm, x_ref), (g_hbm, g_ref)))
    ]
    for copy in copies:
        copy.start()
    for copy in copies:
        copy.wait()
    for k in range(0, subs, 2):
        cols = slice(k * DS, (k + 2) * DS)
        x, g = x_ref[:, cols], g_ref[:, cols]
        out_ref[k] = jnp.concatenate([x[:, :DS], g[:, :DS]], axis=1)
        out_ref[k + 1] = jnp.concatenate([x[:, DS:], g[:, DS:]], axis=1)


def pack(place, x, g, subs):
    rows, width = x.shape[0] // 2, x.shape[1]
    far = lambda v: pltpu.with_memory_space_constraint(v, pltpu.HBM)
    return pl.pallas_call(
        pack_body,
        in_specs=[SCALAR, FAR, FAR],
        out_specs=WHOLE,
        out_shape=jax.ShapeDtypeStruct((subs, rows, LANES), BF16),
        scratch_shapes=[pltpu.VMEM((rows, width), BF16)] * 2 + [pltpu.SemaphoreType.DMA((2,))],
        compiler_params=pltpu.CompilerParams(vmem_limit_bytes=8 * MIB),
        cost_estimate=pl.CostEstimate(flops=10**8, bytes_accessed=2**21, transcendentals=0),
        name="pack",
    )(place, far(x), far(g))


def book_body_prep(place_ref, own_ref, mate_ref, book_ref, bookt_ref):
    width = own_ref.shape[1]
    step = 512
    lane = lax.broadcasted_iota(jnp.int32, (step, LANES), 1)
    for n, ref in enumerate((own_ref, mate_ref)):
        book_ref[:, n * width : (n + 1) * width] = ref[...]
        for c in range(0, width, step):
            v = ref[:, c : c + step].astype(F32)
            turned = jnp.concatenate([v, jnp.zeros_like(v)], axis=0).T
            bookt_ref[n * width + c : n * width + c + step, :] = jnp.where(lane == DS, 1.0, turned).astype(BF16)


def local_pass_body(chunk, parts, xg_ref, book_ref, bookt_ref, *rest):
    e_refs, rest = rest[: len(parts)], rest[len(parts) :]
    ds_hbm, part_ref, dx_ref, stat_ref, xgt_ref, *scratch = rest
    s_slots, m_slots, top_slots, sum_slots, d_slots, ds_slots, e_slots = (scratch[k : k + 2] for k in range(0, 14, 2))
    e_sems, ds_sems = scratch[14:]
    tile, codes = s_slots[0].shape
    tiles = xg_ref.shape[0] // tile
    steps = codes // chunk
    rows = lambda t: span(t * tile, tile)

    def e_at(t, n, c):
        for ref, (first, width, kept, place) in zip(e_refs, parts):
            at = c * chunk - first
            if 0 <= at < width:
                if kept:
                    return ref, (rows(t), slice(at, at + chunk))
                return e_slots[n], (slice(None), slice(place + at, place + at + chunk))

    def e_copies(t, n):
        return [
            pltpu.make_async_copy(e_slots[n].at[:, place : place + width], ref.at[rows(t)], e_sems.at[n, k])
            for k, (ref, (_, width, kept, place)) in enumerate(zip(e_refs, parts))
            if not kept
        ]

    def ds_copy(t, n):
        return pltpu.make_async_copy(ds_slots[n], ds_hbm.at[rows(t)], ds_sems.at[n])

    def look(t, n):
        x = xg_ref[rows(t), :][:, :DS]
        most = None

        def one(c):
            nonlocal most
            if c == steps:
                return
            s = jnp.dot(x, book_ref[:, c * chunk : (c + 1) * chunk], preferred_element_type=F32)
            s_slots[n][:, c * chunk : (c + 1) * chunk] = s
            for k in range(0, chunk, LANES):
                piece = s[:, k : k + LANES]
                most = piece if most is None else jnp.maximum(most, piece)

        def end():
            m_slots[n][...] = most

        return one, end

    def weigh(t, n):
        top = jnp.max(m_slots[n][...], axis=1, keepdims=True) * (SCALE * LOG2E)
        top = jnp.broadcast_to(top, (tile, LANES))
        wide = jnp.concatenate([top] * (chunk // LANES), axis=1)
        acc = jnp.zeros((tile, LANES), F32)

        def one(c):
            nonlocal acc
            if c == steps:
                return
            at = slice(c * chunk, (c + 1) * chunk)
            e = jnp.exp2(s_slots[n][:, at] * (SCALE * LOG2E) - wide).astype(BF16)
            ref, place = e_at(t, n, c)
            ref[place] = e
            acc = acc + jnp.dot(e, bookt_ref[at, :], preferred_element_type=F32)

        def end():
            sum_slots[n][...] = acc
            top_slots[n][...] = top
            for copy in e_copies(t, n):
                copy.start()

        return one, end

    def lean(t, n):
        xg = xg_ref[rows(t), :]
        g = xg[:, DS:]
        sums = sum_slots[n][...]
        lane = lax.broadcasted_iota(jnp.int32, (tile, LANES), 1)
        total = jnp.sum(jnp.where(lane == DS, sums, 0.0), axis=1, keepdims=True)
        h = jnp.sum(sums[:, :DS] * g.astype(F32), axis=1, keepdims=True)
        gq = jnp.broadcast_to(h / total, (tile, LANES))
        wide = jnp.concatenate([gq] * (chunk // LANES), axis=1)
        acc = jnp.zeros((tile, LANES), F32)

        def one(c):
            nonlocal acc
            if c < steps:
                at = slice(c * chunk, (c + 1) * chunk)
                d_slots[c % 2][...] = jnp.dot(g, book_ref[:, at], preferred_element_type=F32) - wide
            if c == 2:
                stat = jnp.where(lane == 0, top_slots[n][...], jnp.where(lane == 1, total, jnp.where(lane == 2, h, gq)))
                stat_ref[:, rows(t)] = stat.T[:4]
                xgt_ref[:, rows(t)] = xg.T
                part_ref[rows(t), :] = jnp.concatenate([sums[:, :DS]] * 2, axis=1)
            if c > 0:
                at = slice((c - 1) * chunk, c * chunk)
                ref, place = e_at(t, n, c - 1)
                ds = (d_slots[(c - 1) % 2][...] * ref[place].astype(F32)).astype(BF16)
                ds_slots[n][:, at] = ds
                acc = acc + jnp.dot(ds, bookt_ref[at, :], preferred_element_type=F32)

        def end():
            dx_ref[rows(t), :] = acc
            ds_copy(t, n).start()

        return one, end

    def wait_e(t, n):
        for copy in e_copies(t, n):
            copy.wait()

    def run(*works):
        for c in range(steps + 1):
            for one, _ in works:
                one(c)
        for _, end in works:
            end()

    run(look(0, 0))
    run(look(1, 1), weigh(0, 0))

    def two(i, carry):
        for n in range(2):
            t = 2 + 2 * i + n
            if n == 0:

                @pl.when(i > 0)
                def _():
                    wait_e(t - 3, 1)
                    ds_copy(t - 4, 0).wait()

            else:
                wait_e(t - 3, 0)

                @pl.when(i > 0)
                def _():
                    ds_copy(t - 4, 1).wait()

            run(look(t, n), weigh(t - 1, 1 - n), lean(t - 2, n))
        return carry

    lax.fori_loop(0, tiles // 2 - 1, two, 0)
    wait_e(tiles - 3, 1)
    ds_copy(tiles - 4, 0).wait()
    run(weigh(tiles - 1, 1), lean(tiles - 2, 0))
    ds_copy(tiles - 3, 1).wait()
    run(lean(tiles - 1, 1))
    wait_e(tiles - 2, 0)
    wait_e(tiles - 1, 1)
    ds_copy(tiles - 2, 0).wait()
    ds_copy(tiles - 1, 1).wait()


def local_pass(xg, book, bookt, parts, tile=128, chunk=1024):
    rows, codes = xg.shape[0], book.shape[1]
    pairs = rows * codes
    staged, placed = 0, []
    for first, width, kept in parts:
        placed.append((first, width, kept, staged))
        staged += 0 if kept else width
    wide, narrow, short = pltpu.VMEM((tile, codes), F32), pltpu.VMEM((tile, LANES), F32), pltpu.VMEM((tile, codes), BF16)
    return pl.pallas_call(
        functools.partial(local_pass_body, chunk, tuple(placed)),
        in_specs=[WHOLE] * 3,
        out_specs=[WHOLE if kept else FAR for _, _, kept in parts] + [FAR] + [WHOLE] * 4,
        out_shape=[(pltpu.VMEM if kept else pltpu.HBM)((rows, width), BF16) for _, width, kept in parts]
        + [
            pltpu.HBM((rows, codes), BF16),
            jax.ShapeDtypeStruct((rows, LANES), F32),
            jax.ShapeDtypeStruct((rows, LANES), F32),
            jax.ShapeDtypeStruct((4, rows), F32),
            jax.ShapeDtypeStruct((LANES, rows), BF16),
        ],
        scratch_shapes=[wide, wide] + [narrow] * 6
        + [pltpu.VMEM((tile, chunk), F32)] * 2
        + [short, short]
        + [pltpu.VMEM((tile, max(staged, LANES)), BF16)] * 2
        + [pltpu.SemaphoreType.DMA((2, len(parts))), pltpu.SemaphoreType.DMA((2,))],
        compiler_params=pltpu.CompilerParams(vmem_limit_bytes=PASS_MIB * MIB),
        cost_estimate=pl.CostEstimate(flops=pairs * 2048, bytes_accessed=pairs * 4, transcendentals=pairs),
        name="local_pass",
    )(xg, book, bookt)


def mix_body(part_ref, dx_ref, xgt_ref, own_ref, o1, o2, o3, out_ref, w_ref):
    rows = part_ref.shape[0]
    stats = [r[...] for r in (own_ref, o1, o2, o3)]
    top = functools.reduce(jnp.maximum, [s[0:1] for s in stats])
    rel = [jnp.exp2(s[0:1] - top) for s in stats]
    z = sum(r * s[1:2] for r, s in zip(rel, stats))
    gq = sum(r * s[2:3] for r, s in zip(rel, stats)) / z
    f_row = rel[0] / z
    off_row = stats[0][3:4] - gq
    x, g = xgt_ref[:DS].astype(F32), xgt_ref[DS:].astype(F32)
    w_ref[:DS] = (x * (SCALE * f_row)).astype(BF16)
    w_ref[DS:] = ((g + (SCALE * off_row) * x) * f_row).astype(BF16)
    step = LANES
    sub = lax.broadcasted_iota(jnp.int32, (8, step), 0)
    lane = lax.broadcasted_iota(jnp.int32, (step, LANES), 1)
    for r in range(0, rows, step):
        at = slice(r, r + step)
        turned = jnp.where(sub == 0, f_row[:, at], off_row[:, at]).T
        f, off = turned[:, 0:1], turned[:, 1:2]
        part = part_ref[at, :]
        dx = dx_ref[at, :][:, :DS]
        lean = (jnp.concatenate([dx, dx], axis=1) + part * off) * SCALE
        out_ref[at, :] = (jnp.where(lane < DS, part, lean) * f).astype(BF16)


def mix(part, dx, xgt, stats):
    rows = part.shape[0]
    return pl.pallas_call(
        mix_body,
        in_specs=[WHOLE] * 7,
        out_specs=[WHOLE] * 2,
        out_shape=[jax.ShapeDtypeStruct((rows, LANES), BF16), jax.ShapeDtypeStruct((LANES, rows), BF16)],
        compiler_params=pltpu.CompilerParams(vmem_limit_bytes=12 * MIB),
        cost_estimate=pl.CostEstimate(flops=10**8, bytes_accessed=2**22, transcendentals=0),
        name="mix",
    )(part, dx, xgt, *stats)


def book_body(first, tile, cuts, w_ref, ds_hbm, e_hbm, out_ref):
    rows, width = e_hbm.shape
    chunk = rows // cuts

    def one(ds_ref, e_ref):
        t, r = pl.program_id(0), pl.program_id(1)
        at = span(t * tile, tile)
        w = w_ref[:, span(r * chunk, chunk)]
        grad = jnp.dot(w[:DS], ds_ref[...], preferred_element_type=F32)
        grad += jnp.dot(w[DS:], e_ref[...], preferred_element_type=F32)
        if cuts == 1:
            out_ref[:, at] = grad
            return

        @pl.when(r == 0)
        def _():
            out_ref[:, at] = grad

        @pl.when(r > 0)
        def _():
            out_ref[:, at] += grad

    specs = [
        pl.BlockSpec((chunk, tile), lambda t, r: (r, first // tile + t)),
        pl.BlockSpec((chunk, tile), lambda t, r: (r, t)),
    ]
    pltpu.emit_pipeline(one, grid=(width // tile, cuts), in_specs=specs)(ds_hbm, e_hbm)


def book_grad(w, ds, e, part):
    first, width, _ = part
    pairs = e.shape[0] * width
    far = lambda v: pltpu.with_memory_space_constraint(v, pltpu.HBM)
    tile, cuts = (1024, 1) if width > 2048 else (512, 1)
    return pl.pallas_call(
        functools.partial(book_body, first, tile, cuts),
        in_specs=[WHOLE, FAR, FAR],
        out_specs=WHOLE,
        out_shape=jax.ShapeDtypeStruct((DS, width), F32),
        compiler_params=pltpu.CompilerParams(vmem_limit_bytes=24 * MIB),
        cost_estimate=pl.CostEstimate(flops=pairs * 1024, bytes_accessed=pairs * 4, transcendentals=0),
        name="book_grad",
    )(w, far(ds), far(e))


def pieces_body(n_z, place_ref, a_ref, own_ref, *send_refs):
    part = own_ref.shape[1]
    for d, out in enumerate((own_ref, *send_refs)):
        out[...] = a_ref[:, span(lax.rem(place_ref[1] + d, n_z) * part, part)]


def sum_body(place_ref, *refs):
    *ins, out = refs
    out[...] = sum(r[...].astype(F32) for r in ins).astype(BF16)


def spread_body(n_z, place_ref, near_1, near_2, from_far, *refs):
    *ins, q_ref, dx_ref, book_ref = refs
    width = near_1.shape[1]
    book_ref[:, :width] = near_1[...] + from_far[:, :width]
    book_ref[:, width:] = near_2[...] + from_far[:, width:]
    subs, part, _ = ins[0].shape
    for n, ref in enumerate(ins):
        swap, d = n // n_z, n % n_z
        core = place_ref[0] if swap == 0 else 1 - place_ref[0]
        at = span((core * n_z + lax.rem(place_ref[1] + n_z - d, n_z)) * part, part)
        for k in range(0, subs, 2):
            a, b = ref[k], ref[k + 1]
            cols = slice(k * DS, (k + 2) * DS)
            q_ref[at, cols] = jnp.concatenate([a[:, :DS], b[:, :DS]], axis=1)
            dx_ref[at, cols] = jnp.concatenate([a[:, DS:], b[:, DS:]], axis=1)


def local(n_sub, n_code, inputs, upstream, codebook):
    n_z = n_code // 2
    index = lax.axis_index("code")
    place = jnp.stack([index % 2, index // 2]).astype(jnp.int32)
    n_rows, width_all = inputs.shape
    mine = n_rows // 2
    shaped = jax.ShapeDtypeStruct
    then = lax.optimization_barrier

    def to_peer(v, d, swap=0):
        pairs = [(j, ((j // 2 + d) % n_z) * 2 + (j % 2 ^ swap)) for j in range(n_code)]
        return lax.ppermute(v, "code", pairs)

    own_book = codebook[0]
    width = own_book.shape[1]
    mate_book = to_peer(own_book, 0, 1)
    xg = pack(place, inputs, upstream, n_sub)
    xg = lax.all_to_all(xg, "sub", 0, 0, tiled=True)
    book, bookt = small(
        book_body_prep, "books", 2, [shaped((DS, 2 * width), BF16), shaped((2 * width, LANES), BF16)], 10**10
    )(place, own_book, mate_book)

    xg = xg.reshape(n_sub * mine, LANES)
    parts = [(width, width, False), (0, width // 2, False), (width // 2, width // 2, False)]
    *es, ds, part, dxl, stat, xgt = local_pass(xg, book, bookt, parts)
    stats = [stat] + [to_peer(stat, d) for d in range(1, n_z)]
    out, w = mix(part, dxl, xgt, stats)

    moved = lax.all_to_all(out.reshape(n_sub, mine, LANES), "sub", 0, 0, tiled=True)
    far = book_grad(w, ds, es[0], parts[0])
    moved, far = then((moved, far))
    from_far = to_peer(far, 0, 1)
    piece = shaped((n_sub, mine // n_z, LANES), BF16)
    own, *sends = small(functools.partial(pieces_body, n_z), "pieces", 1, [piece] * n_z)(place, moved)
    w, own, sends = then((w, own, sends))
    near_1 = book_grad(w, ds, es[1], parts[1])
    got, near_1 = then(([to_peer(v, d) for d, v in enumerate(sends, 1)], near_1))
    (total,) = small(sum_body, "sums", n_z, [piece])(place, own, *got)
    w, total = then((w, total))
    near_2 = book_grad(w, ds, es[2], parts[2])
    ring = [total] + [to_peer(total, d) for d in range(1, n_z)]
    mate_total = to_peer(total, 0, 1)
    ring, mate_total, near_2 = then((ring, mate_total, near_2))
    every = ring + [mate_total] + [to_peer(v, 0, 1) for v in ring[1:]]
    quantized, grads, grad_book = small(
        functools.partial(spread_body, n_z),
        "spread",
        n_code + 3,
        [shaped(inputs.shape, BF16)] * 2 + [shaped((DS, width), F32)],
    )(place, near_1, near_2, from_far, *every)
    return quantized, grads, grad_book[None]


def solution(mesh):
    in_specs = (P("sub", None), P("sub", None), P("sub", None, "code"))
    out_specs = (P("sub", None), P("sub", None), P("sub", None, "code"))
    body = functools.partial(local, mesh.shape["sub"], mesh.shape["code"])
    return jax.shard_map(body, mesh=mesh, in_specs=in_specs, out_specs=out_specs, check_vma=False)
```
